256 devices in a mesh: acq: 4 (over x), tile: 64 (over z, y, core).
Axes of the slice: x: 4, y: 4, z: 8, core: 2. Of those that a mesh axis runs over, the one named last changes fastest.
Arguments:
- slc: bfloat16 [16, 2, 8192, 1280], P('acq', None, 'tile')
- match: int32 [2, 16], replicated, may hold values from 0 to 3, as said below
- dest: int32 [64, 16, 32, 1], P('tile', 'acq'), may hold values from 0 to 3; in each aligned block of 128 rows (0 to 127, 128 to 255, ..., all dimensions but the last counted through in order) at most 64 rows name the same one
- coherent: int32 [64, 16, 32], P('tile', 'acq'), may hold values 0 or 1
Outputs:
- received: bfloat16 [64, 1024, 2, 128], P('tile', 'acq')
The draws below stay inside these ranges and needn't reach their ends.
Inputs may be any that keep to these rules, and one draw needn't show every extreme that they name: `match`: within each round, the entries of each aligned run of 4 acquisitions are a permutation of 0 to 3. `dest`: among the 128 rows of one device, at most 64 name the same owner.
All inputs are finite; a program needn't handle non-finite values. No bound on the sum of `coherent` on one device may be relied on, other than what follows from the above.
Results may differ from the reference program's by a relative error of at most 0.001.
Values may be sent and summed in bfloat16 or wider, within the bound.
No kernel may reach another device: no remote copies, remote signals or barrier semaphores. Data moves between devices by JAX's collectives and lax.ppermute only.
A program may use at most 128 MiB of HBM per device.

```python
import math
import jax
import jax.numpy as jnp
import numpy as np
from jax import lax

ACQ_DEV = 4
PATCH = 32
LOOK_L = 4
LOOK_S = 20
BLOCK_ROWS = 4
PATCH_COLS = 2
ROUNDS = 2
LINES_DEV = 128
SAMPLES_DEV = 1280
ACQ = 16
LINES = 8192
BLOCKS_DEV = 16
BLOCK = 128
ROWS_DEV = 128
CAP = 64
N_ACQ = 4
N_TILE = 64


two_pi = 6.283185307179586


def draw_slc(key, part):
    key = jax.random.fold_in(key, 11)
    keys = jax.random.split(key, 10)
    line_int = jnp.arange(LINES).astype(jnp.int32)
    line_pos = line_int.astype(jnp.float32).reshape(1, LINES, 1)
    line_local = (line_int % LINES_DEV).astype(jnp.float32).reshape(1, LINES, 1)
    tile_float = (line_int // LINES_DEV).astype(jnp.float32).reshape(1, LINES, 1)
    sample_pos = jnp.arange(SAMPLES_DEV).astype(jnp.float32).reshape(1, 1, SAMPLES_DEV)
    ramp = 3.0 ** (0.25 * line_pos / (LINES - 1))
    tile_count = LINES // LINES_DEV
    tile_gain = jnp.exp(0.12 * jax.random.normal(keys[0], (tile_count,), jnp.float32))
    tile_gain = jnp.repeat(tile_gain, LINES_DEV).reshape(1, LINES, 1)
    bright_half = jax.random.randint(keys[1], (), 0, 2).astype(jnp.int32)
    inside = line_int // (LINES // 2) == bright_half
    bright = jnp.where(inside, 1.3, 1.0).astype(jnp.float32).reshape(1, LINES, 1)
    fringe_line = jax.random.uniform(keys[2], (ACQ, 1, 1), jnp.float32, -4.0, 4.0)
    fringe_samp = jax.random.uniform(keys[3], (ACQ, 1, 1), jnp.float32, -3.0, 3.0)
    screen_amp = jax.random.uniform(keys[4], (ACQ, 1, 1), jnp.float32, 1.0, 3.0)
    screen_line = jax.random.uniform(keys[5], (ACQ, 1, 1), jnp.float32, 0.3, 1.0)
    screen_samp = jax.random.uniform(keys[6], (ACQ, 1, 1), jnp.float32, 0.3, 1.5)
    screen_off = jax.random.uniform(keys[7], (ACQ, 1, 1), jnp.float32, -3.14159, 3.14159)
    fringe = two_pi * (fringe_line * line_local / LINES_DEV + fringe_samp * sample_pos / (LOOK_S * PATCH))
    screen_arg = two_pi * (screen_line * line_local / LINES_DEV + screen_samp * sample_pos / SAMPLES_DEV) + screen_off + 1.7 * tile_float
    phase = fringe + screen_amp * jnp.sin(screen_arg)
    cos_phase = jnp.cos(phase)
    sin_phase = jnp.sin(phase)
    common_shape = (2, LINES, SAMPLES_DEV)
    noise_shape = (ACQ, 2, LINES, SAMPLES_DEV)
    common = jnp.clip(jax.random.normal(keys[8], common_shape, jnp.float32), -6.0, 6.0)
    noise = jnp.clip(jax.random.normal(keys[9], noise_shape, jnp.float32), -6.0, 6.0)
    acq_scale = jnp.ones((ACQ, 1, 1), jnp.float32)
    common_real = common[0][None]
    common_imag = common[1][None]
    real_part = 0.6 * (common_real * cos_phase - common_imag * sin_phase) + 0.8 * noise[:, 0]
    imag_part = 0.6 * (common_real * sin_phase + common_imag * cos_phase) + 0.8 * noise[:, 1]
    amplitude = ramp * tile_gain * bright * acq_scale
    values = jnp.stack([real_part * amplitude, imag_part * amplitude], axis=1)
    return values.astype(jnp.bfloat16)


def draw_match(key, part):
    groups = ACQ // ACQ_DEV
    scores = jax.random.randint(jax.random.fold_in(key, 23), (ROUNDS, groups, ACQ_DEV), 0, 1 << 20)
    scores = scores * ACQ_DEV + jnp.arange(ACQ_DEV).astype(jnp.int32)
    order_ids = jnp.argsort(scores, axis=-1, stable=True).astype(jnp.int32)
    return order_ids.reshape(ROUNDS, ACQ)


def touch_ends(array, stream_key, least, largest):
    longest = array.shape.index(max(array.shape))
    spots = []
    for shift in (0, 1):
        where = [jax.random.randint(jax.random.fold_in(stream_key, axis), (), 0, length) for axis, length in enumerate(array.shape)]
        where[longest] = (where[longest] + shift) % array.shape[longest]
        spots.append(tuple(where))
    return array.at[spots[0]].set(least).at[spots[1]].set(largest)


def shared_out(key, own, number, rows, count, top, limit, skew):
    ranking = jax.random.permutation(key, count)
    packed, usual = portions_of(count, rows * top, limit, skew, True), portions_of(count, rows * top, limit, skew, False)
    places = jnp.arange(count)

    def named(lengths, rotation):
        used = int((lengths > 0).sum())
        fixed = max(1, used // 4)
        shifted = fixed + (places - fixed + rotation * (used - fixed)) % max(1, count - fixed)
        return jnp.zeros((count,), jnp.int32).at[ranking[jnp.where(places < fixed, places, shifted)]].set(jnp.asarray(lengths, jnp.int32))

    lengths = jnp.where(number % 4 == 0, named(packed, number // 4), named(usual, number - number // 4 - 1))
    mixed = jax.random.permutation(jax.random.fold_in(own, 3), count)
    giver, taker = mixed[0:count // 2 * 2:2], mixed[1:count // 2 * 2:2]
    room = jnp.minimum(lengths[giver] - 1, limit - lengths[taker]) // 2
    room = jnp.where((giver == ranking[0]) | (taker == ranking[0]) | (lengths[taker] == 0), 0, jnp.maximum(room, 0))
    shifted = jax.random.randint(jax.random.fold_in(own, 4), (count // 2,), 0, 1 << 20) % (room + 1)
    lengths = lengths.at[giver].add(-shifted).at[taker].add(shifted)
    members = jnp.searchsorted(jnp.cumsum(lengths), jnp.arange(rows * top), side="right").astype(jnp.int32)
    grid = members.reshape(top, rows).T
    grid = grid[jax.random.permutation(jax.random.fold_in(own, 1), rows)]
    rotation = jax.random.randint(jax.random.fold_in(own, 2), (rows, 1), 0, top)
    return jnp.take_along_axis(grid, (jnp.arange(top)[None, :] + rotation) % top, axis=1)


def portions_of(count, total, reach, lean, full):
    weights = [(1 << 20) // math.isqrt(standing ** lean) + 1 for standing in range(1, count + 1)]
    largest = reach if full else min(reach, max(-(-total // count), total * weights[0] // sum(weights)))
    least = 1 if total - largest >= count - 1 else 0
    given, surplus = [largest] + [least] * (count - 1), total - largest - least * (count - 1)
    while surplus > 0:
        free = [i for i in range(1, count) if given[i] < largest] or [i for i in range(1, count) if given[i] < reach]
        pool, budget = sum([weights[i] for i in free]), surplus
        for i in free:
            extra = min(reach - given[i], max(1, budget * weights[i] // pool), surplus)
            given[i] = given[i] + extra
            surplus = surplus - extra
    return np.array(given)


def setup_inputs(seed: int = 0) -> dict:
    key_of = jax.random.split(jax.random.key(seed), 5)
    slc = draw_slc(jax.random.fold_in(key_of[4], 71), 0)
    match = draw_match(jax.random.fold_in(key_of[4], 71), 0)
    dest_keys = jax.random.split(jax.random.fold_in(key_of[2], 1), N_TILE * ACQ * (ROUNDS * BLOCKS_DEV) // ROWS_DEV)
    dest_turns = jax.random.permutation(jax.random.fold_in(key_of[2], 3), N_TILE * ACQ * (ROUNDS * BLOCKS_DEV) // ROWS_DEV)
    dest = jax.vmap(lambda own, number: shared_out(jax.random.fold_in(key_of[2], 2), own, number, ROWS_DEV, N_ACQ, 1, CAP, 2))(dest_keys, dest_turns).reshape((N_TILE, ACQ, ROUNDS * BLOCKS_DEV, 1))
    coherent = touch_ends((jax.random.randint(key_of[3], (N_TILE, ACQ, ROUNDS * BLOCKS_DEV), 0, 4) < 3).astype(jnp.int32), jax.random.fold_in(key_of[3], 1), 0, 1)
    return {"slc": slc, "match": match, "dest": dest, "coherent": coherent}


power_floor = 0.25
energy_eps = 1e-06

def reference(slc, match, dest, coherent):
    acq_ids = jnp.arange(ACQ).astype(jnp.int32)
    group_ids = acq_ids // ACQ_DEV
    far_bit = N_ACQ.bit_length() - 2
    partner = jnp.stack([jnp.bitwise_xor(group_ids, 1) * ACQ_DEV + match[0], jnp.bitwise_xor(group_ids, 1 << far_bit) * ACQ_DEV + match[1]]).astype(jnp.int32)

    def looks_one(acq_index):
        own_tile = lax.dynamic_index_in_dim(slc, acq_index, 0, keepdims=False).astype(jnp.float32)
        grids = []
        for round_number in range(ROUNDS):
            other = lax.dynamic_index_in_dim(slc, partner[round_number, acq_index], 0, keepdims=False).astype(jnp.float32)
            real_part = own_tile[0] * other[0] + own_tile[1] * other[1]
            imag_part = own_tile[1] * other[0] - own_tile[0] * other[1]
            stacked = jnp.stack([real_part, imag_part])
            stacked = stacked.reshape(2, LINES // LOOK_L, LOOK_L, SAMPLES_DEV // LOOK_S, LOOK_S)
            grids.append(lax.optimization_barrier(jnp.sum(stacked, axis=(2, 4))) / (LOOK_L * LOOK_S))
        return jnp.stack(grids)
    looked = lax.map(looks_one, acq_ids)
    energy = lax.optimization_barrier(jnp.mean(looked[:, :, 0] ** 2 + looked[:, :, 1] ** 2, axis=(2, 3))) + energy_eps
    field = looked[:, :, 0] + 1j * looked[:, :, 1]
    field = field.reshape(ACQ, ROUNDS, N_TILE, PATCH, PATCH_COLS, PATCH)
    spectrum = jnp.fft.fft2(field, axes=(3, 5))
    scale = energy[:, :, None, None, None, None]
    power = (spectrum.real ** 2 + spectrum.imag ** 2) / (PATCH * PATCH * scale)
    weight = (power + power_floor) ** 0.25
    filtered = jnp.fft.ifft2(weight * spectrum, axes=(3, 5)) / jnp.sqrt(scale)
    parts = jnp.stack([filtered.real, filtered.imag], axis=-1).astype(jnp.float32)
    parts = parts.reshape(ACQ, ROUNDS, N_TILE, PATCH // BLOCK_ROWS, BLOCK_ROWS, PATCH_COLS, PATCH, 2)
    parts = jnp.transpose(parts, (2, 0, 1, 3, 5, 7, 4, 6))
    parts = parts.reshape(N_TILE, ACQ, ROUNDS * BLOCKS_DEV, 2, BLOCK)
    value = (parts * coherent.astype(jnp.float32)[..., None, None]).astype(jnp.bfloat16)
    rows_dev = ACQ_DEV * ROUNDS * BLOCKS_DEV
    value = value.reshape(N_TILE, N_ACQ, rows_dev, 2, BLOCK)
    owner = dest.reshape(N_TILE, N_ACQ, rows_dev)
    onehot = (owner[..., None] == jnp.arange(N_ACQ).astype(jnp.int32)).astype(jnp.int32)
    rank = lax.optimization_barrier(jnp.sum((jnp.cumsum(onehot, axis=2) - onehot) * onehot, axis=-1)).astype(jnp.int32)
    slots = jnp.zeros((N_TILE, N_ACQ, N_ACQ, CAP, 2, BLOCK), jnp.bfloat16)
    tile_ids = jnp.arange(N_TILE).astype(jnp.int32)[:, None, None]
    source_ids = jnp.arange(N_ACQ).astype(jnp.int32)[None, :, None]
    tile_ids = jnp.broadcast_to(tile_ids, owner.shape)
    source_ids = jnp.broadcast_to(source_ids, owner.shape)
    slots = slots.at[tile_ids, owner, source_ids, rank].set(value)
    return slots.reshape(N_TILE, N_ACQ * N_ACQ * CAP, 2, BLOCK)
```

```python
import functools

import jax
import jax.numpy as jnp
import numpy as np
from jax import lax
from jax.experimental import pallas as pl
from jax.experimental.pallas import tpu as pltpu
from jax.sharding import PartitionSpec as P

PATCH = 32
LOOK_L = 4
LOOK_S = 20
BLOCK_ROWS = 4
ROUNDS = 2
ACQ_DEV = 4
SETS = 4
CAP = 64
CHUNKS = 2

power_floor = 0.25
energy_eps = 1e-06


def halves(x):
    head = x.astype(jnp.bfloat16)
    rest = (x - head.astype(np.float64)).astype(jnp.bfloat16)
    return head, rest


def tables(lines):
    k = np.arange(PATCH)
    angle = (k[:, None] * k[None, :] % PATCH) * (2.0 * np.pi / PATCH)
    cosine, sine = np.cos(angle), np.sin(angle)
    width = PATCH * LOOK_S
    looks = (np.arange(width)[:, None] // LOOK_S == np.arange(128)[None, :]).astype(jnp.bfloat16)
    rows = np.concatenate([cosine, sine], 0) / (LOOK_L * LOOK_S * PATCH)
    rows = np.repeat(rows, LOOK_L, axis=1)
    fwd = halves(rows)
    eye = np.eye(4)
    cols = np.concatenate([np.kron(eye, cosine), np.kron(eye, sine)], 1)
    head, rest = halves(cols)
    cols3 = np.concatenate([head, head, rest], 0)
    order = np.arange(PATCH).reshape(PATCH // BLOCK_ROWS, BLOCK_ROWS).T.reshape(-1)
    back = np.concatenate([cosine[order], sine[order]], 0) / PATCH
    head, rest = halves(back)
    back3 = np.concatenate([head, head, rest], 1)
    group = np.kron(eye, np.ones((PATCH, PATCH))).astype(np.float32)
    return looks, fwd, cols3, back3, group


def split(x):
    head = x.astype(jnp.bfloat16)
    return head, (x - head.astype(jnp.float32)).astype(jnp.bfloat16)


def dot(a, b):
    return jnp.dot(a, b, preferred_element_type=jnp.float32)


def forward_chunk(me_ref, match_ref, own, near, far, looks_ref, fwd_ref, prior, pieces):
    lines = own.shape[2]
    me = me_ref[0]
    one, three = me ^ 1, me ^ 3
    total = None
    for j in range(ACQ_DEV):
        pairs = (
            (own, j, near, match_ref[0, me * ACQ_DEV + j]),
            (near, j, own, match_ref[0, one * ACQ_DEV + j]),
            (near, j, far, match_ref[1, one * ACQ_DEV + j]),
            (far, j, near, match_ref[1, three * ACQ_DEV + j]),
        )
        for s, (left, i, right, m) in enumerate(pairs):
            a_re = left[i, 0].astype(jnp.float32)
            a_im = left[i, 1].astype(jnp.float32)
            b_re = right[m, 0].astype(jnp.float32)
            b_im = right[m, 1].astype(jnp.float32)
            re = split(a_re * b_re + a_im * b_im)
            im = split(a_im * b_re - a_re * b_im)
            for h in range(2):
                pieces[j, h, 0, s] = re[h]
                pieces[j, h, 1, s] = im[h]
        width = own.shape[3]
        summed = dot(pieces[j].reshape(2 * 2 * SETS * lines, width), looks_ref[...])
        half = 2 * SETS * lines
        summed = summed[:half] + summed[half:]
        if j:
            summed = pltpu.roll(summed, PATCH * j, 1)
        total = summed if total is None else total + summed
    wide = jnp.concatenate([total[n * lines : (n + 1) * lines] for n in range(2 * SETS)], axis=1)
    head, rest = split(wide)
    both = dot(fwd_ref[...], jnp.concatenate([head, rest, head], axis=0))
    half = SETS * 128
    re = both[:PATCH, :half] + both[PATCH:, half:]
    im = both[:PATCH, half:] - both[PATCH:, :half]
    if prior is not None:
        re, im = re + prior[0], im + prior[1]
    return re, im


def along_columns(re, im, cols_ref, sign):
    tall = jnp.concatenate(
        [x[:, s * 128 : (s + 1) * 128] for x in (re, im) for s in range(SETS)], axis=0
    )
    head, rest = split(tall)
    both = dot(jnp.concatenate([head, rest, head], axis=1), cols_ref[...])
    half = SETS * PATCH
    return (
        both[:half, :128] - sign * both[half:, 128:],
        both[half:, :128] + sign * both[:half, 128:],
    )


def looks_kernel(me_ref, match_ref, own, near, far, looks_ref, fwd_ref, out, pieces):
    re, im = forward_chunk(me_ref, match_ref, own, near, far, looks_ref, fwd_ref, None, pieces)
    out[0] = re
    out[1] = im


def spectrum_kernel(
    me_ref, match_ref, own, near, far, looks_ref, fwd_ref, prior, cols_ref, group_ref, spec, energy, pieces
):
    re, im = forward_chunk(me_ref, match_ref, own, near, far, looks_ref, fwd_ref, prior, pieces)
    re, im = along_columns(re, im, cols_ref, -1.0)
    spec[0] = re
    spec[1] = im
    power = re * re + im * im
    sums = jnp.concatenate(
        [jnp.sum(power[s * PATCH : (s + 1) * PATCH], axis=0, keepdims=True) for s in range(SETS)]
        + [jnp.zeros((8 - SETS, 128), jnp.float32)],
        axis=0,
    )
    sums = jnp.dot(sums, group_ref[...], precision=lax.Precision.HIGHEST, preferred_element_type=jnp.float32)
    lane = lax.broadcasted_iota(jnp.int32, (8, 128), 1) & (PATCH - 1)
    row = lax.broadcasted_iota(jnp.int32, (8, 128), 0)
    energy[0:1] = jnp.sum(jnp.where(lane == row, sums, 0.0), axis=0, keepdims=True)
    energy[1:2] = jnp.sum(jnp.where(lane == (row ^ 1), sums, 0.0), axis=0, keepdims=True)


def filter_kernel(grid_count, spec, parts, cols_ref, back_ref, group_ref, out):
    total = jnp.sum(parts[...], axis=0, keepdims=True)
    lane = lax.broadcasted_iota(jnp.int32, (8, 128), 1) & (PATCH - 1)
    row = lax.broadcasted_iota(jnp.int32, (8, 128), 0)
    spread = jnp.where(lane == row, jnp.broadcast_to(total, (8, 128)), 0.0)
    spread = jnp.dot(spread, group_ref[...], precision=lax.Precision.HIGHEST, preferred_element_type=jnp.float32)
    scale = spread * (1.0 / grid_count) + energy_eps
    inverse = 1.0 / scale
    root = lax.rsqrt(scale)
    re, im = spec[0], spec[1]
    power = re * re + im * im
    power = jnp.concatenate(
        [power[s * PATCH : (s + 1) * PATCH] * inverse[s : s + 1] for s in range(SETS)], axis=0
    )
    weight = jnp.sqrt(jnp.sqrt(power + power_floor))
    re, im = weight * re, weight * im
    re, im = (
        jnp.concatenate([x[s * PATCH : (s + 1) * PATCH] for s in range(SETS)], axis=1) for x in (re, im)
    )
    re, im = along_columns(re, im, cols_ref, 1.0)
    wide = jnp.concatenate([x[s * PATCH : (s + 1) * PATCH] for x in (re, im) for s in range(SETS)], axis=1)
    head, rest = split(wide)
    both = dot(back_ref[...], jnp.concatenate([head, rest, head], axis=0))
    half = SETS * 128
    blocks = PATCH // BLOCK_ROWS
    where = lax.broadcasted_iota(jnp.int32, (blocks, 128), 1) // PATCH
    final = (both[:PATCH, :half] - both[PATCH:, half:], both[:PATCH, half:] + both[PATCH:, :half])
    for part in range(2):
        for s in range(SETS):
            block = final[part][:, s * 128 : (s + 1) * 128] * root[s : s + 1]
            rows = [block[i * blocks : (i + 1) * blocks] for i in range(BLOCK_ROWS)]
            turned = []
            for j in range(ACQ_DEV):
                value = None
                for i in range(BLOCK_ROWS):
                    moved = rows[i] if i == j else pltpu.roll(rows[i], (PATCH * (i - j)) % 128, 1)
                    value = moved if value is None else jnp.where(where == i, moved, value)
                turned.append(value)
            out[s * 32 : (s + 1) * 32, part * 128 : (part + 1) * 128] = jnp.concatenate(
                turned, axis=0
            ).astype(jnp.bfloat16)


VMEM = pl.BlockSpec(memory_space=pltpu.VMEM)
SMEM = pl.BlockSpec(memory_space=pltpu.SMEM)
PARAMS = pltpu.CompilerParams(vmem_limit_bytes=48 * 2**20)


def swapped(x, bits):
    return lax.ppermute(x, "acq", [(i, i ^ bits) for i in range(lax.axis_size("acq"))])


def slot_choice(dest, coherent, me, column):
    rows = dest.size
    n_acq = lax.axis_size("acq")
    owner = dest.reshape(rows)
    onehot = (owner[None, :] == jnp.arange(n_acq)[:, None]).astype(jnp.float32)
    before = (jnp.arange(rows)[:, None] < jnp.arange(rows)[None, :]).astype(jnp.bfloat16)
    counts = jnp.dot(onehot.astype(jnp.bfloat16), before, preferred_element_type=jnp.float32)
    rank = jnp.sum(counts * onehot, axis=0).astype(jnp.int32)
    code = jnp.where(coherent.reshape(rows) > 0, owner * CAP + rank, n_acq * CAP)
    codes = [code] + [swapped(code, bits) for bits in range(1, n_acq)]
    slots = []
    for bits in range(n_acq):
        own_slot = codes[bits] - me * CAP
        own_slot = jnp.where((own_slot >= 0) & (own_slot < CAP), own_slot + (me ^ bits) * CAP, -1)
        slots.append(own_slot.reshape(ACQ_DEV, ROUNDS, PATCH // BLOCK_ROWS, 2))
    lines = []
    for holder in range(n_acq):
        side = column ^ (1 if holder in (1, 2) else 0)
        for bits, turn in ((holder, 0), (holder ^ 1, 0), (holder ^ 1, 1), (holder ^ 3, 1)):
            picked = jnp.where(side == 0, slots[bits][:, turn, :, 0], slots[bits][:, turn, :, 1])
            lines.append(picked.reshape(ACQ_DEV * PATCH // BLOCK_ROWS))
    chosen = jnp.concatenate(lines)
    return (jnp.arange(n_acq * CAP)[:, None] == chosen[None, :]).astype(jnp.bfloat16)


def shards(slc, match, dest, coherent):
    _, _, lines_dev, samples_dev = slc.shape
    n_acq = lax.axis_size("acq")
    n_tile = lax.axis_size("tile")
    grid_count = lines_dev * n_tile // LOOK_L * (samples_dev // LOOK_S)
    me = lax.axis_index("acq").astype(jnp.int32)
    me_arr = me.reshape(1)
    column = 1 - ((me ^ (me >> 1)) & 1)
    looks, (fwd_head, fwd_rest), cols3, back3, group = tables(lines_dev)
    width = samples_dev // 2
    step = lines_dev // CHUNKS

    chunks = []
    for n in range(CHUNKS):
        part = slc[:, :, n * step : (n + 1) * step]
        left, right = part[..., :width], part[..., width:]
        own = jnp.where(column == 0, left, right)
        other = jnp.where(column == 0, right, left)
        chunks.append((own, swapped(other, 1), swapped(own, 3)))

    choice = slot_choice(dest, coherent, me, column)

    prior = None
    for n in range(CHUNKS):
        own, near, far = chunks[n]
        span = slice(n * step, (n + 1) * step)
        fwd3 = np.concatenate([fwd_head[:, span], fwd_head[:, span], fwd_rest[:, span]], axis=1)
        scratch = [pltpu.VMEM((ACQ_DEV, 2, 2, SETS, step, width), jnp.bfloat16)]
        if n < CHUNKS - 1:
            body = looks_kernel if prior is None else more_looks_kernel
            args = [me_arr, match, own, near, far, looks, fwd3] + ([] if prior is None else [prior])
            prior = pl.pallas_call(
                body,
                out_shape=jax.ShapeDtypeStruct((2, PATCH, SETS * 128), jnp.float32),
                in_specs=[SMEM, SMEM] + [VMEM] * (len(args) - 2),
                out_specs=VMEM,
                scratch_shapes=scratch,
                compiler_params=PARAMS,
                name="looks",
            )(*args)
        else:
            spec, energy = pl.pallas_call(
                spectrum_kernel,
                out_shape=(
                    jax.ShapeDtypeStruct((2, SETS * PATCH, 128), jnp.float32),
                    jax.ShapeDtypeStruct((2, 128), jnp.float32),
                ),
                in_specs=[SMEM, SMEM] + [VMEM] * 8,
                out_specs=(VMEM, VMEM),
                scratch_shapes=scratch,
                compiler_params=PARAMS,
                name="spectrum",
            )(me_arr, match, own, near, far, looks, fwd3, prior, cols3, group)

    crossed = energy[1]
    near_energy, far_energy = swapped(crossed, 1), swapped(crossed, 2)
    lane = jnp.arange(128) & (PATCH - 1)
    pair_energy = energy[0] + jnp.where(lane < 2, near_energy, far_energy)
    copies = lax.optimization_barrier(jnp.broadcast_to(pair_energy[None], (n_tile, 128)))
    parts = lax.all_to_all(copies, "tile", split_axis=0, concat_axis=0, tiled=True)

    value = pl.pallas_call(
        functools.partial(filter_kernel, float(grid_count)),
        out_shape=jax.ShapeDtypeStruct((SETS * 32, 256), jnp.bfloat16),
        in_specs=[VMEM] * 5,
        out_specs=VMEM,
        compiler_params=PARAMS,
        name="goldstein",
    )(spec, parts, cols3, back3, group)

    held = [value] + [swapped(value, bits) for bits in range(1, n_acq)]
    held = jnp.concatenate(held, axis=0)
    out = jnp.dot(choice, held, preferred_element_type=jnp.float32).astype(jnp.bfloat16)
    return out.reshape(1, n_acq * CAP, 2, 128)


def more_looks_kernel(me_ref, match_ref, own, near, far, looks_ref, fwd_ref, prior, out, pieces):
    re, im = forward_chunk(me_ref, match_ref, own, near, far, looks_ref, fwd_ref, prior, pieces)
    out[0] = re
    out[1] = im


def solution(mesh):
    return jax.shard_map(
        shards,
        mesh=mesh,
        in_specs=(
            P("acq", None, "tile", None),
            P(),
            P("tile", "acq", None, None),
            P("tile", "acq", None),
        ),
        out_specs=P("tile", "acq", None, None),
        check_vma=False,
    )
```

```python
import functools

import jax
import jax.numpy as jnp
import numpy as np
from jax import lax
from jax.experimental import pallas as pl
from jax.experimental.pallas import tpu as pltpu
from jax.sharding import PartitionSpec as P

PATCH = 32
LOOK_L = 4
LOOK_S = 20
BLOCK_ROWS = 4
ROUNDS = 2
ACQ_DEV = 4
SETS = 4
CAP = 64
CHUNKS = (32, 64, 32)

power_floor = 0.25
energy_eps = 1e-06


def halves(x):
    head = x.astype(jnp.bfloat16)
    rest = (x - head.astype(np.float64)).astype(jnp.bfloat16)
    return head, rest


def tables():
    k = np.arange(PATCH)
    angle = (k[:, None] * k[None, :] % PATCH) * (2.0 * np.pi / PATCH)
    cosine, sine = np.cos(angle), np.sin(angle)
    width = PATCH * LOOK_S
    looks = (np.arange(width)[:, None] // LOOK_S == np.arange(128)[None, :]).astype(jnp.bfloat16)
    rows = np.concatenate([cosine, sine], 0) / (LOOK_L * LOOK_S * PATCH)
    rows = np.repeat(rows, LOOK_L, axis=1)
    fwd = halves(rows)
    eye = np.eye(4)
    cols = np.concatenate([np.kron(eye, cosine), np.kron(eye, sine)], 1)
    head, rest = halves(cols)
    cols3 = np.concatenate([head, head, rest], 0)
    order = np.arange(PATCH).reshape(PATCH // BLOCK_ROWS, BLOCK_ROWS).T.reshape(-1)
    back = np.concatenate([cosine[order], sine[order]], 0) / PATCH
    head, rest = halves(back)
    back3 = np.concatenate([head, head, rest], 1)
    group = np.kron(eye, np.ones((PATCH, PATCH))).astype(np.float32)
    row, place = np.arange(128)[:, None], np.arange(128)[None, :] % 32
    pick = [
        row == place // 8 * 32 + turn * 16 + place % 8 * 2 + side for turn in range(ROUNDS) for side in range(2)
    ]
    pick = np.concatenate(pick, 1).astype(jnp.bfloat16)
    return looks, fwd, cols3, back3, group, pick


def forward_table(head, rest):
    pieces, offsets, first, at = [], [], 0, 0
    for step in CHUNKS:
        span = slice(first, first + step)
        piece = np.concatenate([head[:, span], head[:, span], rest[:, span]], axis=1)
        piece = np.pad(piece, ((0, 0), (0, -piece.shape[1] % 128)))
        pieces.append(piece)
        offsets.append(at)
        first, at = first + step, at + piece.shape[1]
    return np.concatenate(pieces, axis=1), offsets


def split(x):
    head = x.astype(jnp.bfloat16)
    return head, (x - head.astype(jnp.float32)).astype(jnp.bfloat16)


def dot(a, b):
    return jnp.dot(a, b, preferred_element_type=jnp.float32)


def forward_chunk(offset, me_ref, match_ref, own, near, far, looks_ref, fwd_ref, prior, pieces):
    lines = own.shape[2]
    me = me_ref[0]
    one, three = me ^ 1, me ^ 3
    total = None
    for j in range(ACQ_DEV):
        pairs = (
            (own, j, near, match_ref[0, me * ACQ_DEV + j]),
            (near, j, own, match_ref[0, one * ACQ_DEV + j]),
            (near, j, far, match_ref[1, one * ACQ_DEV + j]),
            (far, j, near, match_ref[1, three * ACQ_DEV + j]),
        )
        for s, (left, i, right, m) in enumerate(pairs):
            a_re = left[i, 0].astype(jnp.float32)
            a_im = left[i, 1].astype(jnp.float32)
            b_re = right[m, 0].astype(jnp.float32)
            b_im = right[m, 1].astype(jnp.float32)
            re = split(a_re * b_re + a_im * b_im)
            im = split(a_im * b_re - a_re * b_im)
            for h in range(2):
                pieces[j, h, 0, s] = re[h]
                pieces[j, h, 1, s] = im[h]
        width = own.shape[3]
        summed = dot(pieces[j].reshape(2 * 2 * SETS * lines, width), looks_ref[...])
        half = 2 * SETS * lines
        summed = summed[:half] + summed[half:]
        if j:
            summed = pltpu.roll(summed, PATCH * j, 1)
        total = summed if total is None else total + summed
    wide = jnp.concatenate([total[n * lines : (n + 1) * lines] for n in range(2 * SETS)], axis=1)
    head, rest = split(wide)
    both = dot(fwd_ref[:, offset : offset + 3 * lines], jnp.concatenate([head, rest, head], axis=0))
    half = SETS * 128
    re = both[:PATCH, :half] + both[PATCH:, half:]
    im = both[:PATCH, half:] - both[PATCH:, :half]
    if prior is not None:
        re, im = re + prior[0], im + prior[1]
    return re, im


def along_columns(re, im, cols_ref, sign):
    head, rest = split(jnp.concatenate([re, im], axis=0))
    both = dot(jnp.concatenate([head, rest, head], axis=1), cols_ref[...])
    half = re.shape[0]
    return (
        both[:half, :128] - sign * both[half:, 128:],
        both[half:, :128] + sign * both[:half, 128:],
    )


def looks_kernel(offset, me_ref, match_ref, own, near, far, looks_ref, fwd_ref, *rest):
    prior, out, pieces = rest if len(rest) == 3 else (None, *rest)
    re, im = forward_chunk(offset, me_ref, match_ref, own, near, far, looks_ref, fwd_ref, prior, pieces)
    out[0] = re
    out[1] = im


def spectrum_kernel(
    offset, me_ref, match_ref, own, near, far, looks_ref, fwd_ref, prior, cols_ref, group_ref, code, spec, energy, pieces
):
    re, im = forward_chunk(offset, me_ref, match_ref, own, near, far, looks_ref, fwd_ref, prior, pieces)
    re, im = (
        jnp.concatenate([x[:, s * 128 : (s + 1) * 128] for s in range(SETS)], axis=0) for x in (re, im)
    )
    re, im = along_columns(re, im, cols_ref, -1.0)
    half = SETS * PATCH
    spec[:half] = re
    spec[half : 2 * half] = im
    power = re * re + im * im
    sums = jnp.concatenate(
        [jnp.sum(power[s * PATCH : (s + 1) * PATCH], axis=0, keepdims=True) for s in range(SETS)]
        + [jnp.zeros((8 - SETS, 128), jnp.float32)],
        axis=0,
    )
    sums = jnp.dot(sums, group_ref[...], precision=lax.Precision.HIGHEST, preferred_element_type=jnp.float32)
    lane = lax.broadcasted_iota(jnp.int32, (8, 128), 1) & (PATCH - 1)
    row = lax.broadcasted_iota(jnp.int32, (8, 128), 0)
    mine = jnp.sum(jnp.where(lane == row, sums, 0.0), axis=0, keepdims=True)
    spec[2 * half :] = jnp.broadcast_to(code[...], (8, 128))
    energy[...] = jnp.broadcast_to(mine, energy.shape)


def finish_kernel(grid_count, me_ref, held0, held1, held2, held3, parts, cols_ref, back_ref, group_ref, pick_ref, out, values):
    held = (held0, held1, held2, held3)
    n = len(held)
    me = me_ref[0]
    half = SETS * PATCH
    lane = lax.broadcasted_iota(jnp.int32, (1, 128), 1)
    place = lane & (PATCH - 1)
    n_tile = parts.shape[0] // n
    shares = [
        jnp.sum(parts[pl.ds(pl.multiple_of((me ^ k) * n_tile, 8), n_tile), :], axis=0, keepdims=True)
        for k in range(n)
    ]
    row = lax.broadcasted_iota(jnp.int32, (8, 128), 0)
    spread = []
    for k in range(n):
        other = jnp.where(place < 2, shares[k ^ 1], shares[k ^ 2])
        other = jnp.broadcast_to(other, (8, 128))
        other = jnp.where(lane & 1 == 0, pltpu.roll(other, 127, 1), pltpu.roll(other, 1, 1))
        spread.append(jnp.where(place == row, shares[k] + other, 0.0))
    spread = jnp.concatenate(spread, axis=0)
    spread = jnp.dot(spread, group_ref[...], precision=lax.Precision.HIGHEST, preferred_element_type=jnp.float32)
    scale = spread * (1.0 / grid_count) + energy_eps
    inverse = 1.0 / scale
    root = lax.rsqrt(scale)
    res, ims = [], []
    for k in range(n):
        for s in range(SETS):
            re = held[k][s * PATCH : (s + 1) * PATCH]
            im = held[k][half + s * PATCH : half + (s + 1) * PATCH]
            power = (re * re + im * im) * inverse[8 * k + s : 8 * k + s + 1]
            weight = jnp.sqrt(jnp.sqrt(power + power_floor))
            res.append(weight * re)
            ims.append(weight * im)
    re, im = along_columns(jnp.concatenate(res, axis=0), jnp.concatenate(ims, axis=0), cols_ref, 1.0)
    wide = jnp.concatenate(
        [x[m * PATCH : (m + 1) * PATCH] for x in (re, im) for m in range(n * SETS)], axis=1
    )
    head, rest = split(wide)
    both = dot(back_ref[...], jnp.concatenate([head, rest, head], axis=0))
    whole = n * SETS * 128
    final = (both[:PATCH, :whole] - both[PATCH:, whole:], both[:PATCH, whole:] + both[PATCH:, :whole])
    blocks = PATCH // BLOCK_ROWS
    where = lax.broadcasted_iota(jnp.int32, (blocks, 128), 1) // PATCH
    for part in range(2):
        for m in range(n * SETS):
            at = m // SETS * 8 + m % SETS
            block = final[part][:, m * 128 : (m + 1) * 128] * root[at : at + 1]
            rows = [block[i * blocks : (i + 1) * blocks] for i in range(BLOCK_ROWS)]
            turned = []
            for j in range(ACQ_DEV):
                value = None
                for i in range(BLOCK_ROWS):
                    moved = rows[i] if i == j else pltpu.roll(rows[i], (PATCH * (i - j)) % 128, 1)
                    value = moved if value is None else jnp.where(where == i, moved, value)
                turned.append(value)
            values[m * 32 : (m + 1) * 32, part * 128 : (part + 1) * 128] = jnp.concatenate(
                turned, axis=0
            ).astype(jnp.bfloat16)

    slots = []
    for k in range(n):
        slot = held[k][2 * half : 2 * half + 1].astype(jnp.int32) - me * CAP
        slots.append(jnp.where((slot >= 0) & (slot < CAP), slot + (me ^ k) * CAP, -1))
    slots = jnp.concatenate(slots + slots, axis=0).astype(jnp.float32).astype(jnp.bfloat16)
    picked = dot(slots, pick_ref[...])
    side_me = 1 - ((me ^ (me >> 1)) & 1)
    chosen = []
    for k in range(n):
        side = side_me ^ (1 if k in (1, 2) else 0)
        line = None
        for s, (e, turn) in enumerate(((k, 0), (k ^ 1, 0), (k ^ 1, 1), (k ^ 3, 1))):
            zero = picked[e : e + 1, 2 * turn * 128 : (2 * turn + 1) * 128]
            one = picked[e : e + 1, (2 * turn + 1) * 128 : (2 * turn + 2) * 128]
            both_sides = jnp.where(side == 0, zero, one)
            line = both_sides if line is None else jnp.where(lane // PATCH == s, both_sides, line)
        chosen.append(line)
    chosen = jnp.concatenate(chosen, axis=1).astype(jnp.int32)
    n_slots = n * CAP
    choice = lax.broadcasted_iota(jnp.int32, (n_slots, chosen.shape[1]), 0) == chosen
    choice = jnp.where(choice, 1.0, 0.0).astype(jnp.bfloat16)
    result = dot(choice, values[...])
    out[...] = result.astype(jnp.bfloat16)


VMEM = pl.BlockSpec(memory_space=pltpu.VMEM)
SMEM = pl.BlockSpec(memory_space=pltpu.SMEM)
PARAMS = pltpu.CompilerParams(vmem_limit_bytes=48 * 2**20)


def swapped(x, bits):
    return lax.ppermute(x, "acq", [(i, i ^ bits) for i in range(lax.axis_size("acq"))])


def slot_codes(dest, coherent):
    rows = dest.size
    n_acq = lax.axis_size("acq")
    owner = dest.reshape(rows)
    onehot = (owner[None, :] == jnp.arange(n_acq)[:, None]).astype(jnp.float32)
    before = (jnp.arange(rows)[:, None] < jnp.arange(rows)[None, :]).astype(jnp.bfloat16)
    counts = jnp.dot(onehot.astype(jnp.bfloat16), before, preferred_element_type=jnp.float32)
    rank = jnp.sum(counts * onehot, axis=0).astype(jnp.int32)
    code = jnp.where(coherent.reshape(rows) > 0, owner * CAP + rank, n_acq * CAP)
    return code.astype(jnp.float32).reshape(1, rows)


def shards(slc, match, dest, coherent):
    _, _, lines_dev, samples_dev = slc.shape
    n_acq = lax.axis_size("acq")
    n_tile = lax.axis_size("tile")
    grid_count = lines_dev * n_tile // LOOK_L * (samples_dev // LOOK_S)
    me = lax.axis_index("acq").astype(jnp.int32)
    me_arr = me.reshape(1)
    column = 1 - ((me ^ (me >> 1)) & 1)
    looks, (fwd_head, fwd_rest), cols3, back3, group, pick = tables()
    width = samples_dev // 2

    chunks = []
    first = 0
    for step in CHUNKS:
        if len(chunks) > 1:
            arrived = chunks[-2][2:]
            slc, *arrived = lax.optimization_barrier((slc, *arrived))
            chunks[-2] = chunks[-2][:2] + tuple(arrived)
        part = slc[:, :, first : first + step]
        left, right = part[..., :width], part[..., width:]
        own = jnp.where(column == 0, left, right)
        other = jnp.where(column == 0, right, left)
        own, other, slc, dest, coherent = lax.optimization_barrier((own, other, slc, dest, coherent))
        chunks.append((first, own, swapped(other, 1), swapped(own, 3)))
        first += step

    code = slot_codes(dest, coherent)

    forward, offsets = forward_table(fwd_head, fwd_rest)
    prior = None
    for n, (first, own, near, far) in enumerate(chunks):
        step = own.shape[2]
        scratch = [pltpu.VMEM((ACQ_DEV, 2, 2, SETS, step, width), jnp.bfloat16)]
        args = [me_arr, match, own, near, far, looks, forward] + ([] if prior is None else [prior])
        if n < len(chunks) - 1:
            prior = pl.pallas_call(
                functools.partial(looks_kernel, offsets[n]),
                out_shape=jax.ShapeDtypeStruct((2, PATCH, SETS * 128), jnp.float32),
                in_specs=[SMEM, SMEM] + [VMEM] * (len(args) - 2),
                out_specs=VMEM,
                scratch_shapes=scratch,
                compiler_params=PARAMS,
                name="looks",
            )(*args)
        else:
            spec, energy = pl.pallas_call(
                functools.partial(spectrum_kernel, offsets[n]),
                out_shape=(
                    jax.ShapeDtypeStruct((2 * SETS * PATCH + 8, 128), jnp.float32),
                    jax.ShapeDtypeStruct((n_acq * n_tile, 128), jnp.float32),
                ),
                in_specs=[SMEM, SMEM] + [VMEM] * (len(args) + 1),
                out_specs=(VMEM, VMEM),
                scratch_shapes=scratch,
                compiler_params=PARAMS,
                name="spectrum",
            )(*args, cols3, group, code)

    parts = lax.all_to_all(energy, ("acq", "tile"), split_axis=0, concat_axis=0, tiled=True)
    held = [spec] + [swapped(spec, bits) for bits in range(1, n_acq)]
    out = pl.pallas_call(
        functools.partial(finish_kernel, float(grid_count)),
        out_shape=jax.ShapeDtypeStruct((n_acq * CAP, 256), jnp.bfloat16),
        in_specs=[SMEM] + [VMEM] * 9,
        out_specs=VMEM,
        scratch_shapes=[pltpu.VMEM((n_acq * SETS * 32, 256), jnp.bfloat16)],
        compiler_params=PARAMS,
        name="goldstein",
    )(me_arr, *held, parts, cols3, back3, group, pick)
    return out.reshape(1, n_acq * CAP, 2, 128)


def solution(mesh):
    return jax.shard_map(
        shards,
        mesh=mesh,
        in_specs=(
            P("acq", None, "tile", None),
            P(),
            P("tile", "acq", None, None),
            P("tile", "acq", None),
        ),
        out_specs=P("tile", "acq", None, None),
        check_vma=False,
    )
```

```python
import functools

import jax
import jax.numpy as jnp
import numpy as np
from jax import lax
from jax.experimental import pallas as pl
from jax.experimental.pallas import tpu as pltpu
from jax.sharding import PartitionSpec as P

PATCH = 32
LOOK_L = 4
LOOK_S = 20
BLOCK_ROWS = 4
ROUNDS = 2
ACQ_DEV = 4
SETS = 4
CAP = 64
CHUNKS = (32, 64, 32)

power_floor = 0.25
energy_eps = 1e-06


def halves(x):
    head = x.astype(jnp.bfloat16)
    rest = (x - head.astype(np.float64)).astype(jnp.bfloat16)
    return head, rest


def tables():
    k = np.arange(PATCH)
    angle = (k[:, None] * k[None, :] % PATCH) * (2.0 * np.pi / PATCH)
    cosine, sine = np.cos(angle), np.sin(angle)
    width = PATCH * LOOK_S
    looks = (np.arange(width)[:, None] // LOOK_S == np.arange(128)[None, :]).astype(jnp.bfloat16)
    head, rest = halves(np.concatenate([cosine, sine], 0) / (LOOK_L * LOOK_S * PATCH))
    fwd3 = np.concatenate([head, head, rest], 1)
    eye = np.eye(4)
    cols = np.concatenate([np.kron(eye, cosine), np.kron(eye, sine)], 1)
    head, rest = halves(cols)
    cols3 = np.concatenate([head, head, rest], 0)
    order = np.arange(PATCH).reshape(PATCH // BLOCK_ROWS, BLOCK_ROWS).T.reshape(-1)
    back = np.concatenate([cosine[order], sine[order]], 0) / PATCH
    head, rest = halves(back)
    back3 = np.concatenate([head, head, rest], 1)
    group = np.kron(eye, np.ones((PATCH, PATCH))).astype(np.float32)
    row, place = np.arange(128)[:, None], np.arange(128)[None, :] % 32
    pick = [
        row == place // 8 * 32 + turn * 16 + place % 8 * 2 + side for turn in range(ROUNDS) for side in range(2)
    ]
    pick = np.concatenate(pick, 1).astype(jnp.bfloat16)
    return looks, fwd3, cols3, back3, group, pick


def split(x):
    head = x.astype(jnp.bfloat16)
    return head, (x - head.astype(jnp.float32)).astype(jnp.bfloat16)


def dot(a, b):
    return jnp.dot(a, b, preferred_element_type=jnp.float32)


def look_sums(me_ref, match_ref, own, near, far, looks_ref, products):
    lines = own.shape[2]
    me = me_ref[0]
    one, three = me ^ 1, me ^ 3
    total = None
    for j in range(ACQ_DEV):
        pairs = (
            (own, j, near, match_ref[0, me * ACQ_DEV + j]),
            (near, j, own, match_ref[0, one * ACQ_DEV + j]),
            (near, j, far, match_ref[1, one * ACQ_DEV + j]),
            (far, j, near, match_ref[1, three * ACQ_DEV + j]),
        )
        here = products.at[j % 2]
        for s, (left, i, right, m) in enumerate(pairs):
            a_re = left[i, 0].astype(jnp.float32)
            a_im = left[i, 1].astype(jnp.float32)
            b_re = right[m, 0].astype(jnp.float32)
            b_im = right[m, 1].astype(jnp.float32)
            re = a_re * b_re + a_im * b_im
            im = a_im * b_re - a_re * b_im
            for c in range(here.shape[0]):
                here[c, s * lines : (s + 1) * lines] = re[:, c * 128 : (c + 1) * 128]
                here[c, (SETS + s) * lines : (SETS + s + 1) * lines] = im[:, c * 128 : (c + 1) * 128]
        rows = 2 * SETS * lines // LOOK_L
        looked = []
        for c in range(here.shape[0]):
            x = [here.at[c][pl.ds(i, rows, stride=LOOK_L), :] for i in range(LOOK_L)]
            looked.append((x[0] + x[1]) + (x[2] + x[3]))
        head, rest = split(jnp.concatenate(looked, axis=1))
        summed = dot(jnp.concatenate([head, rest], axis=0), looks_ref[...])
        summed = summed[:rows] + summed[rows:]
        if j:
            summed = pltpu.roll(summed, PATCH * j, 1)
        total = summed if total is None else total + summed
    return total


def along_columns(re, im, cols_ref, sign):
    head, rest = split(jnp.concatenate([re, im], axis=0))
    both = dot(jnp.concatenate([head, rest, head], axis=1), cols_ref[...])
    half = re.shape[0]
    return (
        both[:half, :128] - sign * both[half:, 128:],
        both[half:, :128] + sign * both[:half, 128:],
    )


def looks_kernel(me_ref, match_ref, own, near, far, looks_ref, *rest):
    before, out, products = rest if len(rest) == 3 else (None, *rest)
    looked = look_sums(me_ref, match_ref, own, near, far, looks_ref, products)
    done = 0
    if before is not None:
        done = before.shape[1]
        out[:, :done] = before[...]
    out[:, done:] = looked.reshape(out.shape[0], -1, 128)


def spectrum_kernel(me_ref, match_ref, own, near, far, looks_ref, before, code, fwd_ref, cols_ref, spec, energy, products):
    looked = look_sums(me_ref, match_ref, own, near, far, looks_ref, products)
    n = looked.shape[0]
    rows = n // (2 * SETS)
    sums = []
    for s in range(SETS):
        power = None
        for part in range(2):
            at = part * SETS + s
            for x in (before[at], looked[at * rows : (at + 1) * rows]):
                mean = x * (1.0 / (LOOK_L * LOOK_S))
                mean = jnp.sum(mean * mean, axis=0, keepdims=True)
                power = mean if power is None else power + mean
        sums.append(power)
    sums = jnp.concatenate(sums + [jnp.zeros((8 - SETS, 128), jnp.float32)], axis=0)
    place = lax.broadcasted_iota(jnp.int32, (8, 128), 1) & (PATCH - 1)
    sums = (sums + pltpu.roll(sums, 120, 1)) + (pltpu.roll(sums, 112, 1) + pltpu.roll(sums, 104, 1))
    sums = jnp.where(place < 8, sums, 0.0)
    mine = sums
    for s in range(1, SETS):
        mine = mine + pltpu.roll(pltpu.roll(sums, 8 - s, 0), 8 * s, 1)
    mine = mine[:1]
    energy[...] = jnp.broadcast_to(mine, energy.shape)

    wide = [
        jnp.concatenate([before[at], looked[at * rows : (at + 1) * rows]], axis=0) for at in range(2 * SETS)
    ]
    head, rest = split(jnp.concatenate(wide, axis=1))
    both = dot(fwd_ref[...], jnp.concatenate([head, rest, head], axis=0))
    half = SETS * 128
    re = both[:PATCH, :half] + both[PATCH:, half:]
    im = both[:PATCH, half:] - both[PATCH:, :half]
    re, im = (jnp.concatenate([x[:, s * 128 : (s + 1) * 128] for s in range(SETS)], axis=0) for x in (re, im))
    re, im = along_columns(re, im, cols_ref, -1.0)
    half = SETS * PATCH
    spec[:half] = re
    spec[half : 2 * half] = im
    spec[2 * half :] = jnp.broadcast_to(code[...], (8, 128))


def finish_kernel(grid_count, me_ref, held0, held1, held2, held3, parts, cols_ref, back_ref, group_ref, pick_ref, out, values, woven):
    held = (held0, held1, held2, held3)
    n = len(held)
    me = me_ref[0]
    half = SETS * PATCH
    lane = lax.broadcasted_iota(jnp.int32, (1, 128), 1)
    place = lane & (PATCH - 1)
    n_tile = parts.shape[0] // n
    shares = [
        jnp.sum(parts[pl.ds(pl.multiple_of((me ^ k) * n_tile, 8), n_tile), :], axis=0, keepdims=True)
        for k in range(n)
    ]
    row = lax.broadcasted_iota(jnp.int32, (8, 128), 0)
    spread = []
    for k in range(n):
        other = jnp.where(place < 16, shares[k ^ 1], shares[k ^ 2])
        other = jnp.broadcast_to(other, (8, 128))
        other = jnp.where(lane & 8 == 0, pltpu.roll(other, 120, 1), pltpu.roll(other, 8, 1))
        spread.append(jnp.where(place // 8 == row, shares[k] + other, 0.0))
    spread = jnp.concatenate(spread, axis=0)
    spread = jnp.dot(spread, group_ref[...], precision=lax.Precision.HIGHEST, preferred_element_type=jnp.float32)
    scale = spread * (1.0 / grid_count) + energy_eps
    inverse = 1.0 / scale
    root = lax.rsqrt(scale)
    res, ims = [], []
    for k in range(n):
        for s in range(SETS):
            re = held[k][s * PATCH : (s + 1) * PATCH]
            im = held[k][half + s * PATCH : half + (s + 1) * PATCH]
            power = (re * re + im * im) * inverse[8 * k + s : 8 * k + s + 1]
            weight = lax.rsqrt(lax.rsqrt(power + power_floor))
            res.append(weight * re)
            ims.append(weight * im)
    re, im = along_columns(jnp.concatenate(res, axis=0), jnp.concatenate(ims, axis=0), cols_ref, 1.0)
    wide = jnp.concatenate(
        [x[m * PATCH : (m + 1) * PATCH] for x in (re, im) for m in range(n * SETS)], axis=1
    )
    head, rest = split(wide)
    both = dot(back_ref[...], jnp.concatenate([head, rest, head], axis=0))
    whole = n * SETS * 128
    final = (both[:PATCH, :whole] - both[PATCH:, whole:], both[:PATCH, whole:] + both[PATCH:, :whole])
    blocks = PATCH // BLOCK_ROWS
    where = lax.broadcasted_iota(jnp.int32, (blocks, 128), 1) // PATCH
    for part in range(2):
        for m in range(n * SETS):
            at = m // SETS * 8 + m % SETS
            block = final[part][:, m * 128 : (m + 1) * 128] * root[at : at + 1]
            rows = [block[i * blocks : (i + 1) * blocks] for i in range(BLOCK_ROWS)]
            turned = []
            for j in range(ACQ_DEV):
                value = None
                for i in range(BLOCK_ROWS):
                    moved = rows[i] if i == j else pltpu.roll(rows[i], (PATCH * (i - j)) % 128, 1)
                    value = moved if value is None else jnp.where(where == i, moved, value)
                turned.append(value)
            values[m * 32 : (m + 1) * 32, part * 128 : (part + 1) * 128] = jnp.concatenate(
                turned, axis=0
            ).astype(jnp.bfloat16)

    slots = []
    for k in range(n):
        slot = held[k][2 * half : 2 * half + 1].astype(jnp.int32) - me * CAP
        slots.append(jnp.where((slot >= 0) & (slot < CAP), slot + (me ^ k) * CAP, -1))
    slots = jnp.concatenate(slots + slots, axis=0).astype(jnp.float32).astype(jnp.bfloat16)
    picked = dot(slots, pick_ref[...])
    side_me = 1 - ((me ^ (me >> 1)) & 1)
    chosen = []
    for k in range(n):
        side = side_me ^ (1 if k in (1, 2) else 0)
        line = None
        for s, (e, turn) in enumerate(((k, 0), (k ^ 1, 0), (k ^ 1, 1), (k ^ 3, 1))):
            zero = picked[e : e + 1, 2 * turn * 128 : (2 * turn + 1) * 128]
            one = picked[e : e + 1, (2 * turn + 1) * 128 : (2 * turn + 2) * 128]
            both_sides = jnp.where(side == 0, zero, one)
            line = both_sides if line is None else jnp.where(lane // PATCH == s, both_sides, line)
        chosen.append(line)
    chosen = jnp.concatenate(chosen, axis=1).astype(jnp.int32)
    n_slots = n * CAP
    choice = lax.broadcasted_iota(jnp.int32, (n_slots, chosen.shape[1]), 0) == chosen
    choice = jnp.where(choice, 1.0, 0.0).astype(jnp.bfloat16)
    result = dot(choice, values[...])
    for part in range(2):
        woven[pl.ds(part, n_slots, stride=2), :] = result[:, part * 128 : (part + 1) * 128]
    out[...] = woven[...].astype(jnp.bfloat16)


VMEM = pl.BlockSpec(memory_space=pltpu.VMEM)
SMEM = pl.BlockSpec(memory_space=pltpu.SMEM)
PARAMS = pltpu.CompilerParams(vmem_limit_bytes=48 * 2**20)


def swapped(x, bits):
    return lax.ppermute(x, "acq", [(i, i ^ bits) for i in range(lax.axis_size("acq"))])


def slot_codes(dest, coherent):
    rows = dest.size
    n_acq = lax.axis_size("acq")
    owner = dest.reshape(rows)
    onehot = (owner[None, :] == jnp.arange(n_acq)[:, None]).astype(jnp.float32)
    before = (jnp.arange(rows)[:, None] < jnp.arange(rows)[None, :]).astype(jnp.bfloat16)
    counts = jnp.dot(onehot.astype(jnp.bfloat16), before, preferred_element_type=jnp.float32)
    rank = jnp.sum(counts * onehot, axis=0).astype(jnp.int32)
    code = jnp.where(coherent.reshape(rows) > 0, owner * CAP + rank, n_acq * CAP)
    return code.astype(jnp.float32).reshape(1, rows)


def shards(slc, match, dest, coherent):
    _, _, lines_dev, samples_dev = slc.shape
    n_acq = lax.axis_size("acq")
    n_tile = lax.axis_size("tile")
    grid_count = lines_dev * n_tile // LOOK_L * (samples_dev // LOOK_S)
    me = lax.axis_index("acq").astype(jnp.int32)
    me_arr = me.reshape(1)
    column = 1 - ((me ^ (me >> 1)) & 1)
    looks, fwd3, cols3, back3, group, pick = tables()
    width = samples_dev // 2

    chunks = []
    first = 0
    for step in CHUNKS:
        if len(chunks) > 1:
            arrived = chunks[-2][2:]
            slc, *arrived = lax.optimization_barrier((slc, *arrived))
            chunks[-2] = chunks[-2][:2] + tuple(arrived)
        part = slc[:, :, first : first + step]
        left, right = part[..., :width], part[..., width:]
        own = jnp.where(column == 0, left, right)
        other = jnp.where(column == 0, right, left)
        own, other, slc, dest, coherent = lax.optimization_barrier((own, other, slc, dest, coherent))
        chunks.append((first, own, swapped(other, 1), swapped(own, 3)))
        first += step

    code = slot_codes(dest, coherent)

    before = None
    for n, (first, own, near, far) in enumerate(chunks):
        step = own.shape[2]
        scratch = [pltpu.VMEM((2, width // 128, 2 * SETS * step, 128), jnp.float32)]
        args = [me_arr, match, own, near, far, looks] + ([] if before is None else [before])
        if n < len(chunks) - 1:
            before = pl.pallas_call(
                looks_kernel,
                out_shape=jax.ShapeDtypeStruct((2 * SETS, (first + step) // LOOK_L, 128), jnp.float32),
                in_specs=[SMEM, SMEM] + [VMEM] * (len(args) - 2),
                out_specs=VMEM,
                scratch_shapes=scratch,
                compiler_params=PARAMS,
                name="looks",
            )(*args)
        else:
            spec, energy = pl.pallas_call(
                spectrum_kernel,
                out_shape=(
                    jax.ShapeDtypeStruct((2 * SETS * PATCH + 8, 128), jnp.float32),
                    jax.ShapeDtypeStruct((n_acq * n_tile, 128), jnp.float32),
                ),
                in_specs=[SMEM, SMEM] + [VMEM] * (len(args) + 1),
                out_specs=(VMEM, VMEM),
                scratch_shapes=scratch,
                compiler_params=PARAMS,
                name="spectrum",
            )(*args, code, fwd3, cols3)

    parts = lax.all_to_all(energy, ("acq", "tile"), split_axis=0, concat_axis=0, tiled=True)
    held = [spec] + [swapped(spec, bits) for bits in range(1, n_acq)]
    out = pl.pallas_call(
        functools.partial(finish_kernel, float(grid_count)),
        out_shape=jax.ShapeDtypeStruct((2 * n_acq * CAP, 128), jnp.bfloat16),
        in_specs=[SMEM] + [VMEM] * 9,
        out_specs=VMEM,
        scratch_shapes=[
            pltpu.VMEM((n_acq * SETS * 32, 256), jnp.bfloat16),
            pltpu.VMEM((2 * n_acq * CAP, 128), jnp.float32),
        ],
        compiler_params=PARAMS,
        name="goldstein",
    )(me_arr, *held, parts, cols3, back3, group, pick)
    return out.reshape(1, n_acq * CAP, 2, 128)


def solution(mesh):
    return jax.shard_map(
        shards,
        mesh=mesh,
        in_specs=(
            P("acq", None, "tile", None),
            P(),
            P("tile", "acq", None, None),
            P("tile", "acq", None),
        ),
        out_specs=P("tile", "acq", None, None),
        check_vma=False,
    )
```

```python
import functools

import jax
import jax.numpy as jnp
import numpy as np
from jax import lax
from jax.experimental import pallas as pl
from jax.experimental.pallas import tpu as pltpu
from jax.sharding import PartitionSpec as P

PATCH = 32
LOOK_L = 4
LOOK_S = 20
BLOCK_ROWS = 4
ROUNDS = 2
ACQ_DEV = 4
SETS = 4
CAP = 64
CHUNKS = (32, 64, 32)

power_floor = 0.25
energy_eps = 1e-06


def halves(x):
    head = x.astype(jnp.bfloat16)
    rest = (x - head.astype(np.float64)).astype(jnp.bfloat16)
    return head, rest


def tables():
    k = np.arange(PATCH)
    angle = (k[:, None] * k[None, :] % PATCH) * (2.0 * np.pi / PATCH)
    cosine, sine = np.cos(angle), np.sin(angle)
    width = PATCH * LOOK_S
    looks = (np.arange(width)[:, None] // LOOK_S == np.arange(128)[None, :]).astype(jnp.bfloat16)
    head, rest = halves(np.concatenate([cosine, sine], 0) / (LOOK_L * LOOK_S * PATCH))
    fwd3 = np.concatenate([head, head, rest], 1)
    eye = np.eye(4)
    cols = np.concatenate([np.kron(eye, cosine), np.kron(eye, sine)], 1)
    head, rest = halves(cols)
    cols3 = np.concatenate([head, head, rest], 0)
    order = np.arange(PATCH).reshape(PATCH // BLOCK_ROWS, BLOCK_ROWS).T.reshape(-1)
    back = np.concatenate([cosine[order], sine[order]], 0) / PATCH
    head, rest = halves(back)
    back3 = np.concatenate([head, head, rest], 1)
    group = np.kron(eye, np.ones((PATCH, PATCH))).astype(np.float32)
    row, place = np.arange(128)[:, None], np.arange(128)[None, :] % 32
    pick = [
        row == place // 8 * 32 + turn * 16 + place % 8 * 2 + side for turn in range(ROUNDS) for side in range(2)
    ]
    pick = np.concatenate(pick, 1).astype(jnp.bfloat16)
    return looks, fwd3, cols3, back3, group, pick


def split(x):
    head = x.astype(jnp.bfloat16)
    return head, (x - head.astype(jnp.float32)).astype(jnp.bfloat16)


def dot(a, b):
    return jnp.dot(a, b, preferred_element_type=jnp.float32)


def look_sums(match_ref, own, near, far, looks_ref, products):
    lines = own.shape[2]
    me = lax.axis_index("acq")
    one, three = me ^ 1, me ^ 3
    total = None
    for j in range(ACQ_DEV):
        pairs = (
            (own, j, near, match_ref[0, me * ACQ_DEV + j]),
            (near, j, own, match_ref[0, one * ACQ_DEV + j]),
            (near, j, far, match_ref[1, one * ACQ_DEV + j]),
            (far, j, near, match_ref[1, three * ACQ_DEV + j]),
        )
        here = products.at[j % 2]
        for s, (left, i, right, m) in enumerate(pairs):
            a_re = left[i, 0].astype(jnp.float32)
            a_im = left[i, 1].astype(jnp.float32)
            b_re = right[m, 0].astype(jnp.float32)
            b_im = right[m, 1].astype(jnp.float32)
            re = a_re * b_re + a_im * b_im
            im = a_im * b_re - a_re * b_im
            for c in range(here.shape[0]):
                here[c, s * lines : (s + 1) * lines] = re[:, c * 128 : (c + 1) * 128]
                here[c, (SETS + s) * lines : (SETS + s + 1) * lines] = im[:, c * 128 : (c + 1) * 128]
        rows = 2 * SETS * lines // LOOK_L
        looked = []
        for c in range(here.shape[0]):
            x = [here.at[c][pl.ds(i, rows, stride=LOOK_L), :] for i in range(LOOK_L)]
            looked.append((x[0] + x[1]) + (x[2] + x[3]))
        head, rest = split(jnp.concatenate(looked, axis=1))
        summed = dot(jnp.concatenate([head, rest], axis=0), looks_ref[...])
        summed = summed[:rows] + summed[rows:]
        if j:
            summed = pltpu.roll(summed, PATCH * j, 1)
        total = summed if total is None else total + summed
    return total


def along_columns(re, im, cols_ref, sign):
    head, rest = split(jnp.concatenate([re, im], axis=0))
    both = dot(jnp.concatenate([head, rest, head], axis=1), cols_ref[...])
    half = re.shape[0]
    return (
        both[:half, :128] - sign * both[half:, 128:],
        both[half:, :128] + sign * both[:half, 128:],
    )


def looks_kernel(match_ref, own, near, far, looks_ref, *rest):
    before, out, products = rest if len(rest) == 3 else (None, *rest)
    looked = look_sums(match_ref, own, near, far, looks_ref, products)
    done = 0
    if before is not None:
        done = before.shape[1]
        out[:, :done] = before[...]
    out[:, done:] = looked.reshape(out.shape[0], -1, 128)


def spectrum_kernel(match_ref, own, near, far, looks_ref, before, code, fwd_ref, cols_ref, spec, energy, products):
    looked = look_sums(match_ref, own, near, far, looks_ref, products)
    n = looked.shape[0]
    rows = n // (2 * SETS)
    sums = []
    for s in range(SETS):
        power = None
        for part in range(2):
            at = part * SETS + s
            for x in (before[at], looked[at * rows : (at + 1) * rows]):
                mean = x * (1.0 / (LOOK_L * LOOK_S))
                mean = jnp.sum(mean * mean, axis=0, keepdims=True)
                power = mean if power is None else power + mean
        sums.append(power)
    sums = jnp.concatenate(sums + [jnp.zeros((8 - SETS, 128), jnp.float32)], axis=0)
    place = lax.broadcasted_iota(jnp.int32, (8, 128), 1) & (PATCH - 1)
    sums = (sums + pltpu.roll(sums, 120, 1)) + (pltpu.roll(sums, 112, 1) + pltpu.roll(sums, 104, 1))
    sums = jnp.where(place < 8, sums, 0.0)
    mine = sums
    for s in range(1, SETS):
        mine = mine + pltpu.roll(pltpu.roll(sums, 8 - s, 0), 8 * s, 1)
    mine = mine[:1]
    energy[...] = jnp.broadcast_to(mine, energy.shape)

    wide = [
        jnp.concatenate([before[at], looked[at * rows : (at + 1) * rows]], axis=0) for at in range(2 * SETS)
    ]
    head, rest = split(jnp.concatenate(wide, axis=1))
    both = dot(fwd_ref[...], jnp.concatenate([head, rest, head], axis=0))
    half = SETS * 128
    re = both[:PATCH, :half] + both[PATCH:, half:]
    im = both[:PATCH, half:] - both[PATCH:, :half]
    re, im = (jnp.concatenate([x[:, s * 128 : (s + 1) * 128] for s in range(SETS)], axis=0) for x in (re, im))
    re, im = along_columns(re, im, cols_ref, -1.0)
    half = SETS * PATCH
    spec[:half] = re
    spec[half : 2 * half] = im
    spec[2 * half :] = jnp.broadcast_to(code[...], (8, 128))


def finish_kernel(grid_count, held0, held1, held2, held3, parts, cols_ref, back_ref, group_ref, pick_ref, out, values, woven):
    held = (held0, held1, held2, held3)
    n = len(held)
    me = lax.axis_index("acq")
    half = SETS * PATCH
    lane = lax.broadcasted_iota(jnp.int32, (1, 128), 1)
    place = lane & (PATCH - 1)
    n_tile = parts.shape[0] // n
    shares = [
        jnp.sum(parts[pl.ds(me ^ k, n_tile, stride=n), :], axis=0, keepdims=True)
        for k in range(n)
    ]
    row = lax.broadcasted_iota(jnp.int32, (8, 128), 0)
    spread = []
    for k in range(n):
        other = jnp.where(place < 16, shares[k ^ 1], shares[k ^ 2])
        other = jnp.broadcast_to(other, (8, 128))
        other = jnp.where(lane & 8 == 0, pltpu.roll(other, 120, 1), pltpu.roll(other, 8, 1))
        spread.append(jnp.where(place // 8 == row, shares[k] + other, 0.0))
    spread = jnp.concatenate(spread, axis=0)
    spread = jnp.dot(spread, group_ref[...], precision=lax.Precision.HIGHEST, preferred_element_type=jnp.float32)
    scale = spread * (1.0 / grid_count) + energy_eps
    inverse = 1.0 / scale
    root = lax.rsqrt(scale)
    res, ims = [], []
    for k in range(n):
        for s in range(SETS):
            re = held[k][s * PATCH : (s + 1) * PATCH]
            im = held[k][half + s * PATCH : half + (s + 1) * PATCH]
            power = (re * re + im * im) * inverse[8 * k + s : 8 * k + s + 1]
            weight = lax.rsqrt(lax.rsqrt(power + power_floor))
            res.append(weight * re)
            ims.append(weight * im)
    re, im = along_columns(jnp.concatenate(res, axis=0), jnp.concatenate(ims, axis=0), cols_ref, 1.0)
    wide = jnp.concatenate(
        [x[m * PATCH : (m + 1) * PATCH] for x in (re, im) for m in range(n * SETS)], axis=1
    )
    head, rest = split(wide)
    both = dot(back_ref[...], jnp.concatenate([head, rest, head], axis=0))
    whole = n * SETS * 128
    final = (both[:PATCH, :whole] - both[PATCH:, whole:], both[:PATCH, whole:] + both[PATCH:, :whole])
    blocks = PATCH // BLOCK_ROWS
    where = lax.broadcasted_iota(jnp.int32, (blocks, 128), 1) // PATCH
    for part in range(2):
        for m in range(n * SETS):
            at = m // SETS * 8 + m % SETS
            block = final[part][:, m * 128 : (m + 1) * 128] * root[at : at + 1]
            rows = [block[i * blocks : (i + 1) * blocks] for i in range(BLOCK_ROWS)]
            turned = []
            for j in range(ACQ_DEV):
                value = None
                for i in range(BLOCK_ROWS):
                    moved = rows[i] if i == j else pltpu.roll(rows[i], (PATCH * (i - j)) % 128, 1)
                    value = moved if value is None else jnp.where(where == i, moved, value)
                turned.append(value)
            values[m * 32 : (m + 1) * 32, part * 128 : (part + 1) * 128] = jnp.concatenate(
                turned, axis=0
            ).astype(jnp.bfloat16)

    slots = []
    for k in range(n):
        slot = held[k][2 * half : 2 * half + 1].astype(jnp.int32) - me * CAP
        slots.append(jnp.where((slot >= 0) & (slot < CAP), slot + (me ^ k) * CAP, -1))
    slots = jnp.concatenate(slots + slots, axis=0).astype(jnp.float32).astype(jnp.bfloat16)
    picked = dot(slots, pick_ref[...])
    side_me = 1 - ((me ^ (me >> 1)) & 1)
    chosen = []
    for k in range(n):
        side = side_me ^ (1 if k in (1, 2) else 0)
        line = None
        for s, (e, turn) in enumerate(((k, 0), (k ^ 1, 0), (k ^ 1, 1), (k ^ 3, 1))):
            zero = picked[e : e + 1, 2 * turn * 128 : (2 * turn + 1) * 128]
            one = picked[e : e + 1, (2 * turn + 1) * 128 : (2 * turn + 2) * 128]
            both_sides = jnp.where(side == 0, zero, one)
            line = both_sides if line is None else jnp.where(lane // PATCH == s, both_sides, line)
        chosen.append(line)
    chosen = jnp.concatenate(chosen, axis=1).astype(jnp.int32)
    n_slots = n * CAP
    choice = lax.broadcasted_iota(jnp.int32, (n_slots, chosen.shape[1]), 0) == chosen
    choice = jnp.where(choice, 1.0, 0.0).astype(jnp.bfloat16)
    result = dot(choice, values[...])
    for part in range(2):
        woven[pl.ds(part, n_slots, stride=2), :] = result[:, part * 128 : (part + 1) * 128]
    out[...] = woven[...].astype(jnp.bfloat16)


VMEM = pl.BlockSpec(memory_space=pltpu.VMEM)
SMEM = pl.BlockSpec(memory_space=pltpu.SMEM)
PARAMS = pltpu.CompilerParams(vmem_limit_bytes=48 * 2**20)


def swapped(x, bits):
    return lax.ppermute(x, "acq", [(i, i ^ bits) for i in range(lax.axis_size("acq"))])


def slot_codes(dest, coherent):
    rows = dest.size
    n_acq = lax.axis_size("acq")
    owner = dest.reshape(rows)
    onehot = (owner[None, :] == jnp.arange(n_acq)[:, None]).astype(jnp.float32)
    before = (jnp.arange(rows)[:, None] < jnp.arange(rows)[None, :]).astype(jnp.bfloat16)
    counts = jnp.dot(onehot.astype(jnp.bfloat16), before, preferred_element_type=jnp.float32)
    rank = jnp.sum(counts * onehot, axis=0).astype(jnp.int32)
    code = jnp.where(coherent.reshape(rows) > 0, owner * CAP + rank, n_acq * CAP)
    return code.astype(jnp.float32).reshape(1, rows)


def shards(slc, match, dest, coherent):
    _, _, lines_dev, samples_dev = slc.shape
    n_acq = lax.axis_size("acq")
    n_tile = lax.axis_size("tile")
    grid_count = lines_dev * n_tile // LOOK_L * (samples_dev // LOOK_S)
    me = lax.axis_index("acq").astype(jnp.int32)
    column = 1 - ((me ^ (me >> 1)) & 1)
    looks, fwd3, cols3, back3, group, pick = tables()
    width = samples_dev // 2

    chunks = []
    first = 0
    for step in CHUNKS:
        if len(chunks) > 1:
            arrived = chunks[-2][2:]
            slc, *arrived = lax.optimization_barrier((slc, *arrived))
            chunks[-2] = chunks[-2][:2] + tuple(arrived)
        part = slc[:, :, first : first + step]
        left, right = part[..., :width], part[..., width:]
        own = jnp.where(column == 0, left, right)
        other = jnp.where(column == 0, right, left)
        own, other, slc, dest, coherent = lax.optimization_barrier((own, other, slc, dest, coherent))
        chunks.append((first, own, swapped(other, 1), swapped(own, 3)))
        first += step

    code = slot_codes(dest, coherent)

    before = None
    for n, (first, own, near, far) in enumerate(chunks):
        step = own.shape[2]
        scratch = [pltpu.VMEM((2, width // 128, 2 * SETS * step, 128), jnp.float32)]
        args = [match, own, near, far, looks] + ([] if before is None else [before])
        if n < len(chunks) - 1:
            before = pl.pallas_call(
                looks_kernel,
                out_shape=jax.ShapeDtypeStruct((2 * SETS, (first + step) // LOOK_L, 128), jnp.float32),
                in_specs=[SMEM] + [VMEM] * (len(args) - 1),
                out_specs=VMEM,
                scratch_shapes=scratch,
                compiler_params=PARAMS,
                name="looks",
            )(*args)
        else:
            spec, energy = pl.pallas_call(
                spectrum_kernel,
                out_shape=(
                    jax.ShapeDtypeStruct((2 * SETS * PATCH + 8, 128), jnp.float32),
                    jax.ShapeDtypeStruct((n_acq * n_tile, 128), jnp.float32),
                ),
                in_specs=[SMEM] + [VMEM] * (len(args) + 2),
                out_specs=(VMEM, VMEM),
                scratch_shapes=scratch,
                compiler_params=PARAMS,
                name="spectrum",
            )(*args, code, fwd3, cols3)

    parts = lax.all_to_all(energy, ("tile", "acq"), split_axis=0, concat_axis=0, tiled=True)
    held = [spec] + [swapped(spec, bits) for bits in range(1, n_acq)]
    out = pl.pallas_call(
        functools.partial(finish_kernel, float(grid_count)),
        out_shape=jax.ShapeDtypeStruct((2 * n_acq * CAP, 128), jnp.bfloat16),
        in_specs=[VMEM] * 9,
        out_specs=VMEM,
        scratch_shapes=[
            pltpu.VMEM((n_acq * SETS * 32, 256), jnp.bfloat16),
            pltpu.VMEM((2 * n_acq * CAP, 128), jnp.float32),
        ],
        compiler_params=PARAMS,
        name="goldstein",
    )(*held, parts, cols3, back3, group, pick)
    return out.reshape(1, n_acq * CAP, 2, 128)


def solution(mesh):
    return jax.shard_map(
        shards,
        mesh=mesh,
        in_specs=(
            P("acq", None, "tile", None),
            P(),
            P("tile", "acq", None, None),
            P("tile", "acq", None),
        ),
        out_specs=P("tile", "acq", None, None),
        check_vma=False,
    )
```

```python
import functools

import jax
import jax.numpy as jnp
import numpy as np
from jax import lax
from jax.experimental import pallas as pl
from jax.experimental.pallas import tpu as pltpu
from jax.sharding import PartitionSpec as P

PATCH = 32
LOOK_L = 4
LOOK_S = 20
BLOCK_ROWS = 4
ROUNDS = 2
ACQ_DEV = 4
SETS = 4
CAP = 64
CHUNKS = (32, 64, 32)

power_floor = 0.25
energy_eps = 1e-06


def halves(x):
    head = x.astype(jnp.bfloat16)
    rest = (x - head.astype(np.float64)).astype(jnp.bfloat16)
    return head, rest


def tables():
    k = np.arange(PATCH)
    angle = (k[:, None] * k[None, :] % PATCH) * (2.0 * np.pi / PATCH)
    cosine, sine = np.cos(angle), np.sin(angle)
    width = PATCH * LOOK_S
    looks = (np.arange(width)[:, None] // LOOK_S == np.arange(128)[None, :]).astype(jnp.bfloat16)
    head, rest = halves(np.concatenate([cosine, sine], 0) / (LOOK_L * LOOK_S * PATCH))
    fwd3 = np.concatenate([head, head, rest], 1)
    eye = np.eye(4)
    cols = np.concatenate([np.kron(eye, cosine), np.kron(eye, sine)], 1)
    head, rest = halves(cols)
    cols3 = np.concatenate([head, head, rest], 0)
    order = np.arange(PATCH).reshape(PATCH // BLOCK_ROWS, BLOCK_ROWS).T.reshape(-1)
    back = np.concatenate([cosine[order], sine[order]], 0) / PATCH
    head, rest = halves(back)
    back3 = np.concatenate([head, head, rest], 1)
    group = np.kron(eye, np.ones((PATCH, PATCH))).astype(jnp.bfloat16)
    row, place = np.arange(128)[:, None], np.arange(128)[None, :] % 32
    pick = [
        row == place // 8 * 32 + turn * 16 + place % 8 * 2 + side for turn in range(ROUNDS) for side in range(2)
    ]
    pick = np.concatenate(pick, 1).astype(jnp.bfloat16)
    return looks, fwd3, cols3, back3, group, pick


def split(x):
    head = x.astype(jnp.bfloat16)
    return head, (x - head.astype(jnp.float32)).astype(jnp.bfloat16)


def dot(a, b):
    return jnp.dot(a, b, preferred_element_type=jnp.float32)


def look_sums(match_ref, own, near, far, looks_ref, products):
    lines = own.shape[2]
    me = lax.axis_index("acq")
    one, three = me ^ 1, me ^ 3
    total = None
    for j in range(ACQ_DEV):
        pairs = (
            (own, j, near, match_ref[0, me * ACQ_DEV + j]),
            (near, j, own, match_ref[0, one * ACQ_DEV + j]),
            (near, j, far, match_ref[1, one * ACQ_DEV + j]),
            (far, j, near, match_ref[1, three * ACQ_DEV + j]),
        )
        here = products.at[j % 2]
        for s, (left, i, right, m) in enumerate(pairs):
            a_re = left[i, 0].astype(jnp.float32)
            a_im = left[i, 1].astype(jnp.float32)
            b_re = right[m, 0].astype(jnp.float32)
            b_im = right[m, 1].astype(jnp.float32)
            re = a_re * b_re + a_im * b_im
            im = a_im * b_re - a_re * b_im
            for c in range(here.shape[0]):
                here[c, s * lines : (s + 1) * lines] = re[:, c * 128 : (c + 1) * 128]
                here[c, (SETS + s) * lines : (SETS + s + 1) * lines] = im[:, c * 128 : (c + 1) * 128]
        rows = 2 * SETS * lines // LOOK_L
        looked = []
        for c in range(here.shape[0]):
            x = [here.at[c][pl.ds(i, rows, stride=LOOK_L), :] for i in range(LOOK_L)]
            looked.append((x[0] + x[1]) + (x[2] + x[3]))
        head, rest = split(jnp.concatenate(looked, axis=1))
        summed = dot(jnp.concatenate([head, rest], axis=0), looks_ref[...])
        summed = summed[:rows] + summed[rows:]
        if j:
            summed = pltpu.roll(summed, PATCH * j, 1)
        total = summed if total is None else total + summed
    return total


def along_columns(re, im, cols_ref, sign):
    head, rest = split(jnp.concatenate([re, im], axis=0))
    both = dot(jnp.concatenate([head, rest, head], axis=1), cols_ref[...])
    half = re.shape[0]
    return (
        both[:half, :128] - sign * both[half:, 128:],
        both[half:, :128] + sign * both[:half, 128:],
    )


def looks_kernel(match_ref, own, near, far, looks_ref, *rest):
    before, out, products = rest if len(rest) == 3 else (None, *rest)
    looked = look_sums(match_ref, own, near, far, looks_ref, products)
    done = 0
    if before is not None:
        done = before.shape[1]
        out[:, :done] = before[...]
    out[:, done:] = looked.reshape(out.shape[0], -1, 128)


def spectrum_kernel(match_ref, own, near, far, looks_ref, before, code, fwd_ref, cols_ref, spec, energy, products):
    looked = look_sums(match_ref, own, near, far, looks_ref, products)
    n = looked.shape[0]
    rows = n // (2 * SETS)
    sums = []
    for s in range(SETS):
        power = None
        for part in range(2):
            at = part * SETS + s
            for x in (before[at], looked[at * rows : (at + 1) * rows]):
                mean = x * (1.0 / (LOOK_L * LOOK_S))
                mean = jnp.sum(mean * mean, axis=0, keepdims=True)
                power = mean if power is None else power + mean
        sums.append(power)
    sums = jnp.concatenate(sums + [jnp.zeros((8 - SETS, 128), jnp.float32)], axis=0)
    place = lax.broadcasted_iota(jnp.int32, (8, 128), 1) & (PATCH - 1)
    sums = (sums + pltpu.roll(sums, 120, 1)) + (pltpu.roll(sums, 112, 1) + pltpu.roll(sums, 104, 1))
    sums = jnp.where(place < 8, sums, 0.0)
    mine = sums
    for s in range(1, SETS):
        mine = mine + pltpu.roll(pltpu.roll(sums, 8 - s, 0), 8 * s, 1)
    mine = mine[:1]
    energy[...] = jnp.broadcast_to(mine, energy.shape)

    wide = [
        jnp.concatenate([before[at], looked[at * rows : (at + 1) * rows]], axis=0) for at in range(2 * SETS)
    ]
    head, rest = split(jnp.concatenate(wide, axis=1))
    both = dot(fwd_ref[...], jnp.concatenate([head, rest, head], axis=0))
    half = SETS * 128
    re = both[:PATCH, :half] + both[PATCH:, half:]
    im = both[:PATCH, half:] - both[PATCH:, :half]
    re, im = (jnp.concatenate([x[:, s * 128 : (s + 1) * 128] for s in range(SETS)], axis=0) for x in (re, im))
    re, im = along_columns(re, im, cols_ref, -1.0)
    half = SETS * PATCH
    spec[:half] = re
    spec[half : 2 * half] = im
    spec[2 * half :] = jnp.broadcast_to(code[...], (8, 128))


def finish_kernel(grid_count, held0, held1, held2, held3, parts, cols_ref, back_ref, group_ref, pick_ref, out, values, woven):
    held = (held0, held1, held2, held3)
    n = len(held)
    me = lax.axis_index("acq")
    half = SETS * PATCH
    lane = lax.broadcasted_iota(jnp.int32, (1, 128), 1)
    place = lane & (PATCH - 1)
    n_tile = parts.shape[0] // n
    shares = [
        jnp.sum(parts[pl.ds(me ^ k, n_tile, stride=n), :], axis=0, keepdims=True)
        for k in range(n)
    ]
    row = lax.broadcasted_iota(jnp.int32, (8, 128), 0)
    spread = []
    for k in range(n):
        other = jnp.where(place < 16, shares[k ^ 1], shares[k ^ 2])
        other = jnp.broadcast_to(other, (8, 128))
        other = jnp.where(lane & 8 == 0, pltpu.roll(other, 120, 1), pltpu.roll(other, 8, 1))
        spread.append(jnp.where(place // 8 == row, shares[k] + other, 0.0))
    spread = jnp.concatenate(spread, axis=0)
    head, rest = split(spread)
    spread = dot(jnp.concatenate([head, rest], axis=0), group_ref[...])
    spread = spread[: 8 * n] + spread[8 * n :]
    scale = spread * (1.0 / grid_count) + energy_eps
    inverse = 1.0 / scale
    root = lax.rsqrt(scale)
    res, ims = [], []
    for k in range(n):
        for s in range(SETS):
            re = held[k][s * PATCH : (s + 1) * PATCH]
            im = held[k][half + s * PATCH : half + (s + 1) * PATCH]
            power = (re * re + im * im) * inverse[8 * k + s : 8 * k + s + 1]
            weight = lax.rsqrt(lax.rsqrt(power + power_floor))
            res.append(weight * re)
            ims.append(weight * im)
    re, im = along_columns(jnp.concatenate(res, axis=0), jnp.concatenate(ims, axis=0), cols_ref, 1.0)
    wide = jnp.concatenate(
        [x[m * PATCH : (m + 1) * PATCH] for x in (re, im) for m in range(n * SETS)], axis=1
    )
    head, rest = split(wide)
    both = dot(back_ref[...], jnp.concatenate([head, rest, head], axis=0))
    whole = n * SETS * 128
    final = (both[:PATCH, :whole] - both[PATCH:, whole:], both[:PATCH, whole:] + both[PATCH:, :whole])
    blocks = PATCH // BLOCK_ROWS
    where = lax.broadcasted_iota(jnp.int32, (blocks, 128), 1) // PATCH
    for part in range(2):
        for m in range(n * SETS):
            at = m // SETS * 8 + m % SETS
            block = final[part][:, m * 128 : (m + 1) * 128] * root[at : at + 1]
            rows = [block[i * blocks : (i + 1) * blocks] for i in range(BLOCK_ROWS)]
            turned = []
            for j in range(ACQ_DEV):
                value = None
                for i in range(BLOCK_ROWS):
                    moved = rows[i] if i == j else pltpu.roll(rows[i], (PATCH * (i - j)) % 128, 1)
                    value = moved if value is None else jnp.where(where == i, moved, value)
                turned.append(value)
            values[m * 32 : (m + 1) * 32, part * 128 : (part + 1) * 128] = jnp.concatenate(
                turned, axis=0
            ).astype(jnp.bfloat16)

    slots = []
    for k in range(n):
        slot = held[k][2 * half : 2 * half + 1].astype(jnp.int32) - me * CAP
        slots.append(jnp.where((slot >= 0) & (slot < CAP), slot + (me ^ k) * CAP, -1))
    slots = jnp.concatenate(slots + slots, axis=0).astype(jnp.float32).astype(jnp.bfloat16)
    picked = dot(slots, pick_ref[...])
    side_me = 1 - ((me ^ (me >> 1)) & 1)
    chosen = []
    for k in range(n):
        side = side_me ^ (1 if k in (1, 2) else 0)
        line = None
        for s, (e, turn) in enumerate(((k, 0), (k ^ 1, 0), (k ^ 1, 1), (k ^ 3, 1))):
            zero = picked[e : e + 1, 2 * turn * 128 : (2 * turn + 1) * 128]
            one = picked[e : e + 1, (2 * turn + 1) * 128 : (2 * turn + 2) * 128]
            both_sides = jnp.where(side == 0, zero, one)
            line = both_sides if line is None else jnp.where(lane // PATCH == s, both_sides, line)
        chosen.append(line)
    chosen = jnp.concatenate(chosen, axis=1).astype(jnp.int32)
    n_slots = n * CAP
    choice = lax.broadcasted_iota(jnp.int32, (n_slots, chosen.shape[1]), 0) == chosen
    choice = jnp.where(choice, 1.0, 0.0).astype(jnp.bfloat16)
    result = dot(choice, values[...])
    for part in range(2):
        woven[pl.ds(part, n_slots, stride=2), :] = result[:, part * 128 : (part + 1) * 128]
    out[...] = woven[...].astype(jnp.bfloat16)


VMEM = pl.BlockSpec(memory_space=pltpu.VMEM)
SMEM = pl.BlockSpec(memory_space=pltpu.SMEM)
PARAMS = pltpu.CompilerParams(vmem_limit_bytes=48 * 2**20)


def swapped(x, bits):
    return lax.ppermute(x, "acq", [(i, i ^ bits) for i in range(lax.axis_size("acq"))])


def slot_codes(dest, coherent):
    rows = dest.size
    n_acq = lax.axis_size("acq")
    owner = dest.reshape(rows)
    onehot = (owner[None, :] == jnp.arange(n_acq)[:, None]).astype(jnp.float32)
    before = (jnp.arange(rows)[:, None] < jnp.arange(rows)[None, :]).astype(jnp.bfloat16)
    counts = jnp.dot(onehot.astype(jnp.bfloat16), before, preferred_element_type=jnp.float32)
    rank = jnp.sum(counts * onehot, axis=0).astype(jnp.int32)
    code = jnp.where(coherent.reshape(rows) > 0, owner * CAP + rank, n_acq * CAP)
    return code.astype(jnp.float32).reshape(1, rows)


def shards(slc, match, dest, coherent):
    _, _, lines_dev, samples_dev = slc.shape
    n_acq = lax.axis_size("acq")
    n_tile = lax.axis_size("tile")
    grid_count = lines_dev * n_tile // LOOK_L * (samples_dev // LOOK_S)
    me = lax.axis_index("acq").astype(jnp.int32)
    column = 1 - ((me ^ (me >> 1)) & 1)
    looks, fwd3, cols3, back3, group, pick = tables()
    width = samples_dev // 2

    chunks = []
    first = 0
    for step in CHUNKS:
        if len(chunks) > 1:
            arrived = chunks[-2][2:]
            slc, *arrived = lax.optimization_barrier((slc, *arrived))
            chunks[-2] = chunks[-2][:2] + tuple(arrived)
        part = slc[:, :, first : first + step]
        left, right = part[..., :width], part[..., width:]
        own = jnp.where(column == 0, left, right)
        other = jnp.where(column == 0, right, left)
        own, other, slc, dest, coherent = lax.optimization_barrier((own, other, slc, dest, coherent))
        chunks.append((first, own, swapped(other, 1), swapped(own, 3)))
        first += step

    code = slot_codes(dest, coherent)

    before = None
    for n, (first, own, near, far) in enumerate(chunks):
        step = own.shape[2]
        scratch = [pltpu.VMEM((2, width // 128, 2 * SETS * step, 128), jnp.float32)]
        args = [match, own, near, far, looks] + ([] if before is None else [before])
        if n < len(chunks) - 1:
            before = pl.pallas_call(
                looks_kernel,
                out_shape=jax.ShapeDtypeStruct((2 * SETS, (first + step) // LOOK_L, 128), jnp.float32),
                in_specs=[SMEM] + [VMEM] * (len(args) - 1),
                out_specs=VMEM,
                scratch_shapes=scratch,
                compiler_params=PARAMS,
                name="looks",
            )(*args)
        else:
            spec, energy = pl.pallas_call(
                spectrum_kernel,
                out_shape=(
                    jax.ShapeDtypeStruct((2 * SETS * PATCH + 8, 128), jnp.float32),
                    jax.ShapeDtypeStruct((n_acq * n_tile, 128), jnp.float32),
                ),
                in_specs=[SMEM] + [VMEM] * (len(args) + 2),
                out_specs=(VMEM, VMEM),
                scratch_shapes=scratch,
                compiler_params=PARAMS,
                name="spectrum",
            )(*args, code, fwd3, cols3)

    parts = lax.all_to_all(energy, ("tile", "acq"), split_axis=0, concat_axis=0, tiled=True)
    held = [spec] + [swapped(spec, bits) for bits in range(1, n_acq)]
    out = pl.pallas_call(
        functools.partial(finish_kernel, float(grid_count)),
        out_shape=jax.ShapeDtypeStruct((2 * n_acq * CAP, 128), jnp.bfloat16),
        in_specs=[VMEM] * 9,
        out_specs=VMEM,
        scratch_shapes=[
            pltpu.VMEM((n_acq * SETS * 32, 256), jnp.bfloat16),
            pltpu.VMEM((2 * n_acq * CAP, 128), jnp.float32),
        ],
        compiler_params=PARAMS,
        name="goldstein",
    )(*held, parts, cols3, back3, group, pick)
    return out.reshape(1, n_acq * CAP, 2, 128)


def solution(mesh):
    return jax.shard_map(
        shards,
        mesh=mesh,
        in_specs=(
            P("acq", None, "tile", None),
            P(),
            P("tile", "acq", None, None),
            P("tile", "acq", None),
        ),
        out_specs=P("tile", "acq", None, None),
        check_vma=False,
    )
```
